32 devices in a mesh: seq: 8 (over z, y), grp: 4 (over x, core).
Axes of the slice: x: 2, y: 2, z: 4, core: 2. Of those that a mesh axis runs over, the one named last changes fastest.
Arguments:
- pre_x: bfloat16 [4096, 16384], P('seq', 'grp'), may hold values from -6 to 6
- pre_b: bfloat16 [4096, 2048], P('seq'), may hold values from -6 to 6
- pre_c: bfloat16 [4096, 2048], P('seq'), may hold values from -6 to 6
- pre_dt: float32 [256, 4096], P('grp', 'seq'), may hold values from 0.004 to 0.016
- decay_rate: float32 [256], replicated, may hold values from 0.0078125 to 5
- skip_gain: float32 [256], replicated, may hold values from 0.5 to 1.5
- conv_taps: float32 [4, 20480], replicated, may hold values from -3 to 3
- dec_x: bfloat16 [2, 32, 16384], P(None, 'grp', 'seq'), may hold values from -6 to 6
- dec_b: bfloat16 [2, 32, 2048], P(None, 'grp'), may hold values from -6 to 6
- dec_c: bfloat16 [2, 32, 2048], P(None, 'grp'), may hold values from -6 to 6
- dec_dt: float32 [2, 32, 256], P(None, 'grp', 'seq'), may hold values from 0.004 to 0.016
- dec_query: bfloat16 [2, 32, 8192], P(None, 'grp'), may hold values from -12 to 12
- new_kv: bfloat16 [2, 2, 32, 1024], P(None, None, 'grp'), may hold values from -6 to 6
- cache_kv: bfloat16 [2, 32, 512, 1024], P(None, 'grp', 'seq'), may hold values from -12 to 12
- kv_len: int32 [32], P('grp'), may hold values from 2 to 512, as said below
Outputs:
- pre_y: bfloat16 [4096, 16384], P('seq', 'grp')
- dec_y: bfloat16 [2, 32, 16384], P(None, 'grp', 'seq')
- attn_out: bfloat16 [2, 32, 8192], P(None, 'grp', 'seq')
The draws below stay inside these ranges and needn't reach their ends.
Inputs may be any that keep to these rules, and one draw needn't show every extreme that they name: `kv_len`: row 0 of every group of 8 rows has all 512 positions valid.
All inputs are finite; a program needn't handle non-finite values.
Results may differ from the reference program's by a relative error of at most 0.0013.
Values sent between devices are 32-bit elements; how exact they have to be, the bound alone decides.
A program may use at most 128 MiB of HBM per device.

```python
import math
import jax
import jax.numpy as jnp
from jax import lax

HEADS = 256
HDIM = 64
STATE = 256
GROUPS = 8
TAPS = 4
QHEADS = 64
KVHEADS = 8
ADIM = 128
SPAN = 256
STEPS = 2
ROWS_GRP = 8
PROMPT = 4096
ROWS = 32
CACHE = 512


def draw_dec_query(key, part):
    drawn = jax.random.truncated_normal(jax.random.fold_in(key, 11), -6.0, 6.0, (STEPS, ROWS, QHEADS * ADIM), jnp.float32)
    return drawn.astype(jnp.bfloat16)


def draw_cache_kv(key, part):
    drawn = jax.random.truncated_normal(jax.random.fold_in(key, 12), -6.0, 6.0, (2, ROWS, CACHE, KVHEADS * ADIM), jnp.float32)
    return drawn.astype(jnp.bfloat16)


def draw_kv_len(key, part):
    lengths = jax.random.randint(jax.random.fold_in(key, 13), (ROWS,), 2, CACHE + 1)
    row_ids = jnp.arange(ROWS)
    return jnp.where(row_ids % ROWS_GRP == 0, CACHE, lengths).astype(jnp.int32)


def steps_of(key, extent, pieces, smallest, top_value):
    def one(axis_at, shards_of):
        draws = jax.random.uniform(jax.random.fold_in(jax.random.fold_in(key, 6), axis_at), (shards_of,), jnp.float32, smallest / len(pieces), top_value / len(pieces))
        return jnp.repeat(jnp.exp(draws), extent[axis_at] // shards_of).reshape((-1,) + (1,) * (len(extent) - axis_at - 1))

    level = one(*pieces[0])
    for cut in pieces[1:]:
        level = level * one(*cut)
    return level


def scatter_about(key, extent, deviation, limit, shards=(), kind=jnp.bfloat16):
    gain = steps_of(key, extent, shards, -0.22, 0.18) if shards else 1.0
    values = jax.random.normal(key, extent, jnp.float32) * deviation * gain
    return jnp.minimum(jnp.maximum(values, -limit), limit).astype(kind)


def setup_inputs(seed: int = 0) -> dict:
    key_list = jax.random.split(jax.random.key(seed), 16)
    return {
        "pre_x": scatter_about(key_list[0], (PROMPT, HEADS * HDIM), 1.0, 6.0, ((0, 8), (1, 4))),
        "pre_b": scatter_about(key_list[1], (PROMPT, GROUPS * STATE), 1.0, 6.0, ((0, 8),)),
        "pre_c": scatter_about(key_list[2], (PROMPT, GROUPS * STATE), 1.0, 6.0, ((0, 8),)),
        "pre_dt": jnp.clip(jnp.exp(math.log(0.016) - 1.3862944 * jax.random.uniform(key_list[3], (HEADS, PROMPT), jnp.float32) ** steps_of(key_list[3], (HEADS, PROMPT), ((0, 4), (1, 8)), -0.2, 0.2)), 0.004, 0.016),
        "decay_rate": jnp.clip(jnp.exp(jax.random.uniform(key_list[4], (HEADS,), jnp.float32, math.log(0.0078125), math.log(5.0))), 0.0078125, 5.0),
        "skip_gain": jnp.clip(1.0 + 0.1 * jax.random.normal(key_list[5], (HEADS,), jnp.float32), 0.5, 1.5),
        "conv_taps": scatter_about(key_list[6], (TAPS, HEADS * HDIM + 2 * GROUPS * STATE), 0.5, 3.0, (), jnp.float32),
        "dec_x": scatter_about(key_list[7], (STEPS, ROWS, HEADS * HDIM), 1.0, 6.0, ((1, 4), (2, 8))),
        "dec_b": scatter_about(key_list[8], (STEPS, ROWS, GROUPS * STATE), 1.0, 6.0, ((1, 4),)),
        "dec_c": scatter_about(key_list[9], (STEPS, ROWS, GROUPS * STATE), 1.0, 6.0, ((1, 4),)),
        "dec_dt": jnp.clip(jnp.exp(math.log(0.016) - 1.3862944 * jax.random.uniform(key_list[10], (STEPS, ROWS, HEADS), jnp.float32) ** steps_of(key_list[10], (STEPS, ROWS, HEADS), ((1, 4), (2, 8)), -0.2, 0.2)), 0.004, 0.016),
        "dec_query": draw_dec_query(jax.random.fold_in(key_list[15], 71), 0),
        "new_kv": scatter_about(key_list[12], (2, STEPS, ROWS, KVHEADS * ADIM), 1.0, 6.0, ((2, 4),)),
        "cache_kv": draw_cache_kv(jax.random.fold_in(key_list[15], 71), 0),
        "kv_len": draw_kv_len(jax.random.fold_in(key_list[15], 71), 0),
    }


HIGH = lax.Precision.HIGHEST
NEG = -1.0e30


def causal_conv(leading, source, kernel):
    row_total = source.shape[0]
    padded = jnp.concatenate([leading, source], axis=0)
    accumulated = jnp.zeros_like(source)
    for position in range(TAPS):
        accumulated = accumulated + kernel[position] * padded[position:position + row_total]
    return jax.nn.silu(accumulated)


def decode_conv(leading, fresh, kernel):
    results = []
    for current in range(fresh.shape[0]):
        accumulated = jnp.zeros(fresh.shape[1:], jnp.float32)
        for position in range(TAPS):
            place = current + position
            if place < TAPS - 1:
                term = leading[place][None, :]
            else:
                term = fresh[place - (TAPS - 1)]
            accumulated = accumulated + kernel[position] * term
        results.append(jax.nn.silu(accumulated))
    return jnp.stack(results)


def span_pass(ssm_state, block):
    inputs, entries, readout, log_decay = block
    cumulative = jnp.cumsum(log_decay, axis=1)
    block_size = log_decay.shape[1]
    causal = jnp.arange(block_size)[:, None] >= jnp.arange(block_size)[None, :]
    spreads = cumulative[:, :, None] - cumulative[:, None, :]
    weights = jnp.where(causal[None], jnp.exp(jnp.where(causal[None], spreads, 0.0)), 0.0)
    intersection = jnp.dot(readout, entries.T, precision=HIGH)
    intra_span = jnp.einsum('kts,skp->tkp', weights * intersection[None], inputs, precision=HIGH)
    carried = jnp.exp(cumulative).T[:, :, None] * jnp.einsum('tn,kpn->tkp', readout, ssm_state, precision=HIGH)
    remaining = jnp.exp(cumulative[:, -1:] - cumulative)
    updates = jnp.einsum('skp,sn->kpn', inputs * remaining.T[:, :, None], entries, precision=HIGH)
    renewed = jnp.exp(cumulative[:, -1])[:, None, None] * ssm_state + updates
    return renewed, intra_span + carried


def run_spans(inputs, entries, readout, log_decay, ssm_state):
    row_total, heads_here, head_width = inputs.shape
    block_total = row_total // SPAN
    blocks = (inputs.reshape(block_total, SPAN, heads_here, head_width),
              entries.reshape(block_total, SPAN, entries.shape[1]),
              readout.reshape(block_total, SPAN, readout.shape[1]),
              log_decay.reshape(heads_here, block_total, SPAN).transpose(1, 0, 2))
    ssm_state, results = lax.scan(span_pass, ssm_state, blocks)
    return results.reshape(row_total, heads_here, head_width), ssm_state


def decode_mamba(ssm_state, heads_x, heads_b, heads_c, step_dt, rates, gains):
    decays = jnp.exp(-step_dt * rates)
    from_prefix = jnp.einsum('jrhn,hpn->jrhp', heads_c, ssm_state, precision=HIGH)
    results = []
    for current in range(heads_x.shape[0]):
        factor = jnp.ones(decays.shape[1:], jnp.float32)
        accumulated = gains[None, :, None] * heads_x[current]
        for earlier in range(current, -1, -1):
            intersection = jnp.sum(heads_c[current] * heads_b[earlier], axis=-1)
            accumulated = accumulated + (factor * step_dt[earlier] * intersection)[..., None] * heads_x[earlier]
            factor = factor * decays[earlier]
        accumulated = accumulated + factor[..., None] * from_prefix[current]
        results.append(accumulated)
    return jnp.stack(results)


def reference(pre_x, pre_b, pre_c, pre_dt, decay_rate, skip_gain, conv_taps, dec_x, dec_b, dec_c, dec_dt, dec_query, new_kv, cache_kv, kv_len):
    per_group = HEADS // GROUPS
    edge = TAPS - 1
    x_offset = HEADS * HDIM
    c_offset = HEADS * HDIM + GROUPS * STATE

    def one_group(group_id):
        source_x = lax.dynamic_slice_in_dim(pre_x, group_id * per_group * HDIM, per_group * HDIM, 1).astype(jnp.float32)
        source_b = lax.dynamic_slice_in_dim(pre_b, group_id * STATE, STATE, 1).astype(jnp.float32)
        source_c = lax.dynamic_slice_in_dim(pre_c, group_id * STATE, STATE, 1).astype(jnp.float32)
        kernel_x = lax.dynamic_slice_in_dim(conv_taps, group_id * per_group * HDIM, per_group * HDIM, 1)
        kernel_b = lax.dynamic_slice_in_dim(conv_taps, x_offset + group_id * STATE, STATE, 1)
        kernel_c = lax.dynamic_slice_in_dim(conv_taps, c_offset + group_id * STATE, STATE, 1)
        conv_x = causal_conv(jnp.zeros((edge, per_group * HDIM), jnp.float32), source_x, kernel_x)
        conv_b = causal_conv(jnp.zeros((edge, STATE), jnp.float32), source_b, kernel_b)
        conv_c = causal_conv(jnp.zeros((edge, STATE), jnp.float32), source_c, kernel_c)
        step_sizes = lax.dynamic_slice_in_dim(pre_dt, group_id * per_group, per_group, 0)
        rates = lax.dynamic_slice_in_dim(decay_rate, group_id * per_group, per_group, 0)
        gains = lax.dynamic_slice_in_dim(skip_gain, group_id * per_group, per_group, 0)
        log_decay = -step_sizes * rates[:, None]
        head_inputs = conv_x.reshape(PROMPT, per_group, HDIM)
        scaled = head_inputs * step_sizes.T[:, :, None]
        blank = jnp.zeros((per_group, HDIM, STATE), jnp.float32)
        results, closing = run_spans(scaled, conv_b, conv_c, log_decay, blank)
        outputs = results + gains[None, :, None] * head_inputs
        return outputs.reshape(PROMPT, per_group * HDIM).astype(jnp.bfloat16), closing

    group_ids = jnp.arange(GROUPS, dtype=jnp.int32)
    stacked_y, closings = lax.map(one_group, group_ids)
    pre_y = stacked_y.transpose(1, 0, 2).reshape(PROMPT, HEADS * HDIM)
    prefix_state = closings.reshape(HEADS, HDIM, STATE)

    tail_x = pre_x[PROMPT - edge:].astype(jnp.float32)
    tail_b = pre_b[PROMPT - edge:].astype(jnp.float32)
    tail_c = pre_c[PROMPT - edge:].astype(jnp.float32)
    step_x = decode_conv(tail_x, dec_x.astype(jnp.float32), conv_taps[:, :x_offset])
    step_b = decode_conv(tail_b, dec_b.astype(jnp.float32), conv_taps[:, x_offset:c_offset])
    step_c = decode_conv(tail_c, dec_c.astype(jnp.float32), conv_taps[:, c_offset:])
    heads_x = step_x.reshape(STEPS, ROWS, HEADS, HDIM)
    heads_b = jnp.repeat(step_b.reshape(STEPS, ROWS, GROUPS, STATE), per_group, axis=2)
    heads_c = jnp.repeat(step_c.reshape(STEPS, ROWS, GROUPS, STATE), per_group, axis=2)
    mamba_out = decode_mamba(prefix_state, heads_x, heads_b, heads_c, dec_dt, decay_rate, skip_gain)
    dec_y = mamba_out.reshape(STEPS, ROWS, HEADS * HDIM).astype(jnp.bfloat16)

    group_size = QHEADS // KVHEADS
    score_scale = ADIM ** -0.5

    def attend_row(packed):
        query_row, cached_keys, cached_values, fresh_keys, fresh_values, valid_length = packed
        queries = query_row.astype(jnp.float32).reshape(STEPS, KVHEADS, group_size, ADIM)
        key_rows = cached_keys.astype(jnp.float32).reshape(CACHE, KVHEADS, ADIM)
        value_rows = cached_values.astype(jnp.float32).reshape(CACHE, KVHEADS, ADIM)
        new_keys = fresh_keys.astype(jnp.float32).reshape(STEPS, KVHEADS, ADIM)
        new_values = fresh_values.astype(jnp.float32).reshape(STEPS, KVHEADS, ADIM)
        cache_scores = jnp.einsum('jkgd,ckd->jkgc', queries, key_rows, precision=HIGH) * score_scale
        usable = (jnp.arange(CACHE) < valid_length)[None, None, None, :]
        cache_scores = jnp.where(usable, cache_scores, NEG)
        new_scores = jnp.einsum('jkgd,ikd->jkgi', queries, new_keys, precision=HIGH) * score_scale
        allowed = (jnp.arange(STEPS)[None, :] <= jnp.arange(STEPS)[:, None])[:, None, None, :]
        new_scores = jnp.where(allowed, new_scores, NEG)
        peak_score = jnp.maximum(jnp.max(cache_scores, axis=-1), jnp.max(new_scores, axis=-1))
        cache_weights = jnp.where(usable, jnp.exp(cache_scores - peak_score[..., None]), 0.0)
        new_weights = jnp.where(allowed, jnp.exp(new_scores - peak_score[..., None]), 0.0)
        weight_sum = jnp.sum(cache_weights, axis=-1) + jnp.sum(new_weights, axis=-1)
        summed = jnp.einsum('jkgc,ckd->jkgd', cache_weights, value_rows, precision=HIGH)
        summed = summed + jnp.einsum('jkgi,ikd->jkgd', new_weights, new_values, precision=HIGH)
        return (summed / weight_sum[..., None]).reshape(STEPS, QHEADS * ADIM)

    packed_rows = (dec_query.transpose(1, 0, 2), cache_kv[0], cache_kv[1],
                   new_kv[0].transpose(1, 0, 2), new_kv[1].transpose(1, 0, 2), kv_len)
    attended = lax.map(attend_row, packed_rows)
    attn_out = attended.transpose(1, 0, 2).astype(jnp.bfloat16)
    return pre_y, dec_y, attn_out
```

```python
import functools

import jax
import jax.numpy as jnp
from jax import lax
from jax.experimental import pallas as pl
from jax.experimental.pallas import tpu as pltpu
from jax.sharding import PartitionSpec as P

HEADS = 256
HDIM = 64
STATE = 256
GROUPS = 8
TAPS = 4
QHEADS = 64
KVHEADS = 8
ADIM = 128
SPAN = 256
STEPS = 2


HIGH = lax.Precision.HIGH
MESH = pl.DeviceIdType.MESH
NEG = -1e30


def passed_along(value, axis, steps):
    count = lax.axis_size(axis)
    first, last = (max(0, -steps), min(count, count - steps))
    return lax.ppermute(value, axis, [(source, source + steps) for source in range(first, last)])


def from_root(value, axis, source):
    kept = jnp.where(lax.axis_index(axis) == source, value, 0).astype(value.dtype)
    return lax.psum(kept, axis)


def causal_conv(leading, source, kernel):
    row_total = source.shape[0]
    padded = jnp.concatenate([leading, source], axis=0)
    accumulated = jnp.zeros_like(source)
    for position in range(TAPS):
        accumulated = accumulated + kernel[position] * padded[position : position + row_total]
    return jax.nn.silu(accumulated)


def decode_conv(leading, fresh, kernel):
    results = []
    for current in range(fresh.shape[0]):
        accumulated = jnp.zeros(fresh.shape[1:], jnp.float32)
        for position in range(TAPS):
            place = current + position
            if place < TAPS - 1:
                term = leading[place][None, :]
            else:
                term = fresh[place - (TAPS - 1)]
            accumulated = accumulated + kernel[position] * term
        results.append(jax.nn.silu(accumulated))
    return jnp.stack(results)


def span_pass(ssm_state, block):
    inputs, entries, readout, log_decay = block
    cumulative = jnp.cumsum(log_decay, axis=1)
    block_size = log_decay.shape[1]
    causal = jnp.arange(block_size)[:, None] >= jnp.arange(block_size)[None, :]
    spreads = cumulative[:, :, None] - cumulative[:, None, :]
    weights = jnp.where(causal[None], jnp.exp(jnp.where(causal[None], spreads, 0.0)), 0.0)
    intersection = jnp.dot(readout, entries.T, precision=HIGH)
    intra_span = jnp.einsum("kts,skp->tkp", weights * intersection[None], inputs, precision=HIGH)
    carried = jnp.exp(cumulative).T[:, :, None] * jnp.einsum(
        "tn,kpn->tkp", readout, ssm_state, precision=HIGH
    )
    remaining = jnp.exp(cumulative[:, -1:] - cumulative)
    updates = jnp.einsum("skp,sn->kpn", inputs * remaining.T[:, :, None], entries, precision=HIGH)
    renewed = jnp.exp(cumulative[:, -1])[:, None, None] * ssm_state + updates
    return (renewed, intra_span + carried)


def run_spans(inputs, entries, readout, log_decay, ssm_state):
    row_total, heads_here, head_width = inputs.shape
    block_total = row_total // SPAN
    blocks = (
        inputs.reshape(block_total, SPAN, heads_here, head_width),
        entries.reshape(block_total, SPAN, entries.shape[1]),
        readout.reshape(block_total, SPAN, readout.shape[1]),
        log_decay.reshape(heads_here, block_total, SPAN).transpose(1, 0, 2),
    )
    ssm_state, results = lax.scan(span_pass, ssm_state, blocks)
    return (results.reshape(row_total, heads_here, head_width), ssm_state)


def decode_mamba(ssm_state, heads_x, heads_b, heads_c, step_dt, rates, gains):
    decays = jnp.exp(-step_dt * rates)
    from_prefix = jnp.einsum("jrhn,hpn->jrhp", heads_c, ssm_state, precision=HIGH)
    results = []
    for current in range(heads_x.shape[0]):
        factor = jnp.ones(decays.shape[1:], jnp.float32)
        accumulated = gains[None, :, None] * heads_x[current]
        for earlier in range(current, -1, -1):
            intersection = jnp.sum(heads_c[current] * heads_b[earlier], axis=-1)
            accumulated = (
                accumulated
                + (factor * step_dt[earlier] * intersection)[..., None] * heads_x[earlier]
            )
            factor = factor * decays[earlier]
        accumulated = accumulated + factor[..., None] * from_prefix[current]
        results.append(accumulated)
    return jnp.stack(results)


def group_layout(head_begin, head_count):
    per_group = HEADS // GROUPS
    group_count = max(1, head_count // per_group)
    return (head_begin // per_group, group_count, head_count // group_count)


def relay_kernel(
    count,
    groups,
    chunk,
    factor_ref,
    local_ref,
    incoming_ref,
    prefix_ref,
    leaving,
    send_sem,
    recv_sem,
    final_send,
    prefix_recv,
    fan_send,
):
    me = lax.axis_index("seq")
    mine = lax.axis_index("grp")
    local_heads = local_ref.shape[0]
    state_heads = prefix_ref.shape[0]
    shares = local_heads // state_heads
    pieces = local_heads // chunk
    own_pieces = state_heads // chunk
    last = count - 1
    is_last = me == last
    is_root = me // shares == mine

    barrier = pltpu.get_barrier_semaphore()

    def greet(where):
        pl.semaphore_signal(barrier, inc=1, device_id=where, device_id_type=MESH)

    @pl.when(me > 0)
    def _():
        greet((me - 1, mine))

    @pl.when(me < last)
    def _():
        greet((me + 1, mine))

    for other in range(1, groups):
        greet((me, lax.rem(mine + other, groups)))

    @pl.when(jnp.logical_and(is_root, me < last))
    def _():
        greet((last, mine))

    for share in range(shares):
        owner = mine * shares + share

        @pl.when(jnp.logical_and(is_last, owner != last))
        def _():
            greet((owner, mine))

    expected = (
        (me > 0).astype(jnp.int32)
        + (me < last).astype(jnp.int32)
        + (groups - 1)
        + jnp.logical_and(is_root, me < last).astype(jnp.int32)
    )
    for share in range(shares):
        expected = expected + jnp.logical_and(is_last, mine * shares + share != last).astype(
            jnp.int32
        )
    pl.semaphore_wait(barrier, expected)

    def pass_on(piece, target):
        rows = pl.ds(piece * chunk, chunk)
        return pltpu.make_async_remote_copy(
            src_ref=leaving.at[rows],
            dst_ref=incoming_ref.at[rows],
            send_sem=send_sem.at[piece],
            recv_sem=recv_sem.at[piece],
            device_id=(target, mine),
            device_id_type=MESH,
        )

    def final_copy(piece, own_piece, owner):
        return pltpu.make_async_remote_copy(
            src_ref=leaving.at[pl.ds(piece * chunk, chunk)],
            dst_ref=prefix_ref.at[pl.ds(own_piece * chunk, chunk)],
            send_sem=final_send.at[piece],
            recv_sem=prefix_recv.at[own_piece],
            device_id=(owner, mine),
            device_id_type=MESH,
        )

    def fan_copy(own_piece, other):
        rows = pl.ds(own_piece * chunk, chunk)
        return pltpu.make_async_remote_copy(
            src_ref=prefix_ref.at[rows],
            dst_ref=prefix_ref.at[rows],
            send_sem=fan_send.at[other - 1, own_piece],
            recv_sem=prefix_recv.at[own_piece],
            device_id=(me, lax.rem(mine + other, groups)),
            device_id_type=MESH,
        )

    def one_piece(piece, carry):
        rows = pl.ds(piece * chunk, chunk)

        @pl.when(me == 0)
        def _():
            incoming_ref[rows] = jnp.zeros((chunk,) + local_ref.shape[1:], jnp.float32)

        @pl.when(me > 0)
        def _():
            pass_on(piece, me).wait_recv()

        for head in range(chunk):
            at = piece * chunk + head
            leaving[at] = factor_ref[at] * incoming_ref[at] + local_ref[at]

        @pl.when(me < last)
        def _():
            pass_on(piece, me + 1).start()

        owner = mine * shares + piece // own_pieces
        own_piece = lax.rem(piece, own_pieces)

        @pl.when(jnp.logical_and(is_last, owner != last))
        def _():
            final_copy(piece, own_piece, owner).start()

        @pl.when(jnp.logical_and(is_last, owner == last))
        def _():
            prefix_ref[pl.ds(own_piece * chunk, chunk)] = leaving[rows]
            for other in range(1, groups):
                fan_copy(own_piece, other).start()

        return carry

    lax.fori_loop(0, pieces, one_piece, 0)

    def one_arrival(own_piece, carry):
        @pl.when(jnp.logical_not(jnp.logical_and(is_root, is_last)))
        def _():
            final_copy(own_piece, own_piece, me).wait_recv()

        @pl.when(jnp.logical_and(is_root, me < last))
        def _():
            for other in range(1, groups):
                fan_copy(own_piece, other).start()

        return carry

    lax.fori_loop(0, own_pieces, one_arrival, 0)

    def drain(piece, carry):
        owner = mine * shares + piece // own_pieces

        @pl.when(me < last)
        def _():
            pass_on(piece, me).wait_send()

        @pl.when(jnp.logical_and(is_last, owner != last))
        def _():
            final_copy(piece, lax.rem(piece, own_pieces), owner).wait_send()

        return carry

    lax.fori_loop(0, pieces, drain, 0)

    @pl.when(is_root)
    def _():
        def drain_fan(own_piece, carry):
            for other in range(1, groups):
                fan_copy(own_piece, other).wait_send()
            return carry

        lax.fori_loop(0, own_pieces, drain_fan, 0)


def relay_states(factor, local_state, state_heads, count, groups):
    local_heads = local_state.shape[0]
    chunk = 2
    pieces = local_heads // chunk
    own_pieces = state_heads // chunk
    vmem = pl.BlockSpec(memory_space=pltpu.VMEM)
    return pl.pallas_call(
        functools.partial(relay_kernel, count, groups, chunk),
        out_shape=(
            jax.ShapeDtypeStruct(local_state.shape, jnp.float32),
            jax.ShapeDtypeStruct((state_heads,) + local_state.shape[1:], jnp.float32),
        ),
        in_specs=[pl.BlockSpec(memory_space=pltpu.SMEM), vmem],
        out_specs=(vmem, vmem),
        scratch_shapes=[
            pltpu.VMEM(local_state.shape, jnp.float32),
            pltpu.SemaphoreType.DMA((pieces,)),
            pltpu.SemaphoreType.DMA((pieces,)),
            pltpu.SemaphoreType.DMA((pieces,)),
            pltpu.SemaphoreType.DMA((own_pieces,)),
            pltpu.SemaphoreType.DMA((groups - 1, own_pieces)),
        ],
        compiler_params=pltpu.CompilerParams(
            collective_id=0, has_side_effects=True, vmem_limit_bytes=40 * 1024 * 1024
        ),
    )(factor, local_state)


def on_device(
    pre_x,
    pre_b,
    pre_c,
    pre_dt,
    decay_rate,
    skip_gain,
    conv_taps,
    dec_x,
    dec_b,
    dec_c,
    dec_dt,
    dec_query,
    new_kv,
    cache_kv,
    kv_len,
):
    seq_count = lax.axis_size("seq")
    seq_index = lax.axis_index("seq")
    grp_index = lax.axis_index("grp")
    section = pre_x.shape[0]
    local_heads = pre_x.shape[1] // HDIM
    edge = TAPS - 1
    x_offset = HEADS * HDIM
    c_offset = HEADS * HDIM + GROUPS * STATE
    head_begin = grp_index * local_heads
    group_begin, group_count, heads_each = group_layout(head_begin, local_heads)
    source_x = pre_x.astype(jnp.float32)
    full_b = pre_b.astype(jnp.float32)
    full_c = pre_c.astype(jnp.float32)
    own_b = lax.dynamic_slice_in_dim(full_b, group_begin * STATE, group_count * STATE, 1)
    own_c = lax.dynamic_slice_in_dim(full_c, group_begin * STATE, group_count * STATE, 1)
    edge_rows = jnp.concatenate(
        [source_x[section - edge :], own_b[section - edge :], own_c[section - edge :]], axis=1
    )
    edge_rows = passed_along(edge_rows, "seq", 1)
    split_b = local_heads * HDIM
    split_c = split_b + group_count * STATE
    leading = (edge_rows[:, :split_b], edge_rows[:, split_b:split_c], edge_rows[:, split_c:])
    is_end = seq_index == seq_count - 1
    shown_x = jnp.where(is_end, source_x[section - edge :], 0.0)
    shown_bc = jnp.where(
        jnp.logical_and(is_end, grp_index == 0),
        jnp.concatenate([full_b[section - edge :], full_c[section - edge :]], axis=1),
        0.0,
    )
    tails = jnp.concatenate([jnp.zeros((edge, x_offset), jnp.float32), shown_bc], axis=1)
    tails = lax.dynamic_update_slice_in_dim(tails, shown_x, head_begin * HDIM, 1)
    tails = lax.psum(tails, ("seq", "grp"))
    kernel_x = lax.dynamic_slice_in_dim(conv_taps, head_begin * HDIM, local_heads * HDIM, 1)
    kernel_b = lax.dynamic_slice_in_dim(
        conv_taps, x_offset + group_begin * STATE, group_count * STATE, 1
    )
    kernel_c = lax.dynamic_slice_in_dim(
        conv_taps, c_offset + group_begin * STATE, group_count * STATE, 1
    )
    conv_x = causal_conv(leading[0], source_x, kernel_x)
    conv_b = causal_conv(leading[1], own_b, kernel_b)
    conv_c = causal_conv(leading[2], own_c, kernel_c)
    rates = lax.dynamic_slice_in_dim(decay_rate, head_begin, local_heads, 0)
    gains = lax.dynamic_slice_in_dim(skip_gain, head_begin, local_heads, 0)
    log_decay = -pre_dt * rates[:, None]
    head_inputs = conv_x.reshape(section, local_heads, HDIM)
    scaled = head_inputs * pre_dt.T[:, :, None]
    grouped = scaled.reshape(section, group_count, heads_each, HDIM).transpose(1, 0, 2, 3)
    entries = conv_b.reshape(section, group_count, STATE).transpose(1, 0, 2)
    readout = conv_c.reshape(section, group_count, STATE).transpose(1, 0, 2)
    decay_groups = log_decay.reshape(group_count, heads_each, section)
    blank = jnp.zeros((group_count, heads_each, HDIM, STATE), jnp.float32)
    intra_part, closing_local = jax.vmap(run_spans)(grouped, entries, readout, decay_groups, blank)
    local_state = closing_local.reshape(local_heads, HDIM, STATE)
    cumulative = jnp.cumsum(log_decay, axis=1)
    section_decay = cumulative[:, -1]

    state_heads = HEADS // seq_count
    incoming, prefix_state = relay_states(
        jnp.exp(section_decay), local_state, state_heads, seq_count, lax.axis_size("grp")
    )
    incoming_groups = incoming.reshape(group_count, heads_each, HDIM, STATE)
    from_before = jnp.einsum("gsn,gkpn->gskp", readout, incoming_groups, precision=HIGH)
    decay_factor = jnp.exp(cumulative).reshape(group_count, heads_each, section).transpose(0, 2, 1)
    combined = intra_part + decay_factor[..., None] * from_before
    combined = (
        combined.transpose(1, 0, 2, 3).reshape(section, local_heads, HDIM)
        + gains[None, :, None] * head_inputs
    )
    pre_y = combined.reshape(section, local_heads * HDIM).astype(jnp.bfloat16)
    prefix_tail = lax.dynamic_slice_in_dim(
        tails, seq_index * state_heads * HDIM, state_heads * HDIM, 1
    )
    tail_b = tails[:, x_offset:c_offset]
    tail_c = tails[:, c_offset:]
    rows_here = dec_x.shape[1]
    dec_begin = seq_index * state_heads
    dgroup_begin, dgroup_count, dheads_each = group_layout(dec_begin, state_heads)
    kernel_dx = lax.dynamic_slice_in_dim(conv_taps, dec_begin * HDIM, state_heads * HDIM, 1)
    kernel_db = lax.dynamic_slice_in_dim(
        conv_taps, x_offset + dgroup_begin * STATE, dgroup_count * STATE, 1
    )
    kernel_dc = lax.dynamic_slice_in_dim(
        conv_taps, c_offset + dgroup_begin * STATE, dgroup_count * STATE, 1
    )
    step_x = decode_conv(prefix_tail, dec_x.astype(jnp.float32), kernel_dx)
    step_b = decode_conv(
        lax.dynamic_slice_in_dim(tail_b, dgroup_begin * STATE, dgroup_count * STATE, 1),
        lax.dynamic_slice_in_dim(dec_b, dgroup_begin * STATE, dgroup_count * STATE, 2).astype(
            jnp.float32
        ),
        kernel_db,
    )
    step_c = decode_conv(
        lax.dynamic_slice_in_dim(tail_c, dgroup_begin * STATE, dgroup_count * STATE, 1),
        lax.dynamic_slice_in_dim(dec_c, dgroup_begin * STATE, dgroup_count * STATE, 2).astype(
            jnp.float32
        ),
        kernel_dc,
    )
    heads_x = step_x.reshape(STEPS, rows_here, state_heads, HDIM)
    heads_b = jnp.repeat(step_b.reshape(STEPS, rows_here, dgroup_count, STATE), dheads_each, axis=2)
    heads_c = jnp.repeat(step_c.reshape(STEPS, rows_here, dgroup_count, STATE), dheads_each, axis=2)
    dec_rates = lax.dynamic_slice_in_dim(decay_rate, dec_begin, state_heads, 0)
    dec_gains = lax.dynamic_slice_in_dim(skip_gain, dec_begin, state_heads, 0)
    mamba_out = decode_mamba(prefix_state, heads_x, heads_b, heads_c, dec_dt, dec_rates, dec_gains)
    dec_y = mamba_out.reshape(STEPS, rows_here, state_heads * HDIM).astype(jnp.bfloat16)
    group_size = QHEADS // KVHEADS
    score_scale = ADIM ** (-0.5)
    positions = cache_kv.shape[2]
    queries = dec_query.reshape(STEPS, rows_here, KVHEADS, group_size, ADIM)
    key_rows = cache_kv[0].reshape(rows_here, positions, KVHEADS, ADIM)
    value_rows = cache_kv[1].reshape(rows_here, positions, KVHEADS, ADIM).astype(jnp.float32)
    scores = (
        jnp.einsum("jrkgd,rckd->jrkgc", queries, key_rows, preferred_element_type=jnp.float32)
        * score_scale
    )
    places = seq_index * positions + jnp.arange(positions)
    usable = (places[None, :] < kv_len[:, None])[None, :, None, None, :]
    scores = jnp.where(usable, scores, NEG)
    peak_local = jnp.max(scores, axis=-1)
    weights = jnp.where(usable, jnp.exp(scores - peak_local[..., None]), 0.0)
    mass_local = jnp.sum(weights, axis=-1)
    summed_local = jnp.einsum("jrkgc,rckd->jrkgd", weights, value_rows, precision=HIGH)
    peak_local = peak_local.reshape(STEPS, rows_here, QHEADS)
    mass_local = mass_local.reshape(STEPS, rows_here, QHEADS)
    summed_local = summed_local.reshape(STEPS, rows_here, QHEADS, ADIM)
    own_heads = QHEADS // seq_count
    head_start = seq_index * own_heads
    pieces = (
        lax.all_to_all(peak_local[None], "seq", split_axis=3, concat_axis=0, tiled=True),
        lax.all_to_all(mass_local[None], "seq", split_axis=3, concat_axis=0, tiled=True),
        lax.all_to_all(summed_local[None], "seq", split_axis=3, concat_axis=0, tiled=True),
    )
    peak_cache = jnp.max(pieces[0], axis=0)
    rescale = jnp.exp(pieces[0] - peak_cache[None])
    mass_cache = jnp.sum(pieces[1] * rescale, axis=0)
    summed_cache = jnp.sum(pieces[2] * rescale[..., None], axis=0)
    new_keys = new_kv[0].reshape(STEPS, rows_here, KVHEADS, ADIM)
    new_values = new_kv[1].reshape(STEPS, rows_here, KVHEADS, ADIM).astype(jnp.float32)
    new_scores = (
        jnp.einsum("jrkgd,irkd->jrkgi", queries, new_keys, preferred_element_type=jnp.float32)
        * score_scale
    )
    allowed = (jnp.arange(STEPS)[None, :] <= jnp.arange(STEPS)[:, None])[:, None, None, None, :]
    new_scores = jnp.where(allowed, new_scores, NEG)
    new_scores = lax.dynamic_slice_in_dim(
        new_scores.reshape(STEPS, rows_here, QHEADS, STEPS), head_start, own_heads, 2
    )
    allowed_heads = (jnp.arange(STEPS)[None, :] <= jnp.arange(STEPS)[:, None])[:, None, None, :]
    head_kv = (head_start + jnp.arange(own_heads)) // group_size
    pick = (head_kv[:, None] == jnp.arange(KVHEADS)[None, :]).astype(jnp.float32)
    own_values = jnp.einsum("hk,irkd->irhd", pick, new_values, precision=HIGH)
    peak_total = jnp.maximum(peak_cache, jnp.max(new_scores, axis=-1))
    cache_scale = jnp.exp(peak_cache - peak_total)
    new_weights = jnp.where(allowed_heads, jnp.exp(new_scores - peak_total[..., None]), 0.0)
    mass_total = mass_cache * cache_scale + jnp.sum(new_weights, axis=-1)
    summed_total = summed_cache * cache_scale[..., None] + jnp.einsum(
        "jrhi,irhd->jrhd", new_weights, own_values, precision=HIGH
    )
    attn_out = (
        (summed_total / mass_total[..., None])
        .reshape(STEPS, rows_here, own_heads * ADIM)
        .astype(jnp.bfloat16)
    )
    return (pre_y, dec_y, attn_out)


def solution(mesh):
    in_specs = (
        P("seq", "grp"),
        P("seq", None),
        P("seq", None),
        P("grp", "seq"),
        P(),
        P(),
        P(),
        P(None, "grp", "seq"),
        P(None, "grp", None),
        P(None, "grp", None),
        P(None, "grp", "seq"),
        P(None, "grp", None),
        P(None, None, "grp", None),
        P(None, "grp", "seq", None),
        P("grp"),
    )
    out_specs = (P("seq", "grp"), P(None, "grp", "seq"), P(None, "grp", "seq"))
    return jax.shard_map(
        on_device, mesh=mesh, in_specs=in_specs, out_specs=out_specs, check_vma=False
    )
```

```python
import functools

import jax
import jax.numpy as jnp
from jax import lax
from jax.experimental import pallas as pl
from jax.experimental.pallas import tpu as pltpu
from jax.sharding import PartitionSpec as P

HEADS = 256
HDIM = 64
STATE = 256
GROUPS = 8
TAPS = 4
QHEADS = 64
KVHEADS = 8
ADIM = 128
SPAN = 256
STEPS = 2


HIGH = lax.Precision.HIGH
MESH = pl.DeviceIdType.MESH
NEG = -1e30
PAIR = 2 * HDIM


def passed_along(value, axis, steps):
    count = lax.axis_size(axis)
    first, last = (max(0, -steps), min(count, count - steps))
    return lax.ppermute(value, axis, [(source, source + steps) for source in range(first, last)])


def causal_conv(leading, source, kernel):
    row_total = source.shape[0]
    padded = jnp.concatenate([leading, source], axis=0)
    accumulated = jnp.zeros_like(source)
    for position in range(TAPS):
        accumulated = accumulated + kernel[position] * padded[position : position + row_total]
    return jax.nn.silu(accumulated)


def decode_conv(leading, fresh, kernel):
    results = []
    for current in range(fresh.shape[0]):
        accumulated = jnp.zeros(fresh.shape[1:], jnp.float32)
        for position in range(TAPS):
            place = current + position
            if place < TAPS - 1:
                term = leading[place][None, :]
            else:
                term = fresh[place - (TAPS - 1)]
            accumulated = accumulated + kernel[position] * term
        results.append(jax.nn.silu(accumulated))
    return jnp.stack(results)


def decode_mamba(from_prefix, heads_x, heads_b, heads_c, step_dt, rates, gains):
    decays = jnp.exp(-step_dt * rates)
    results = []
    for current in range(heads_x.shape[0]):
        factor = jnp.ones(decays.shape[1:], jnp.float32)
        accumulated = gains[None, :, None] * heads_x[current]
        for earlier in range(current, -1, -1):
            intersection = jnp.sum(heads_c[current] * heads_b[earlier], axis=-1)
            accumulated = (
                accumulated
                + (factor * step_dt[earlier] * intersection)[..., None] * heads_x[earlier]
            )
            factor = factor * decays[earlier]
        accumulated = accumulated + factor[..., None] * from_prefix[current]
        results.append(accumulated)
    return jnp.stack(results)


def group_layout(head_begin, head_count):
    per_group = HEADS // GROUPS
    group_count = max(1, head_count // per_group)
    return (head_begin // per_group, group_count, head_count // group_count)


def split(value):
    hi = value.astype(jnp.bfloat16)
    return hi, (value - hi.astype(jnp.float32)).astype(jnp.bfloat16)


def split_outside(value):
    hi = lax.reduce_precision(value, 8, 7)
    return hi.astype(jnp.bfloat16), (value - hi).astype(jnp.bfloat16)


def dot_split(hi, lo, right):
    right_hi, right_lo = split(right)
    width = right.shape[1]
    both = jnp.dot(
        hi,
        jnp.concatenate([right_hi, right_lo], axis=1),
        preferred_element_type=jnp.float32,
    )
    small = jnp.dot(lo, right_hi, preferred_element_type=jnp.float32)
    return both[:, :width] + (both[:, width:] + small)


def relay_kernel(
    count,
    groups,
    x_ref,
    lead_ref,
    taps_ref,
    rows_ref,
    lanes_ref,
    bt_hi_ref,
    bt_lo_ref,
    c_hi_ref,
    c_lo_ref,
    cb_ref,
    y_ref,
    prefix_ref,
    incoming_ref,
    leaving,
    padded,
    send_sem,
    recv_sem,
    final_send,
    prefix_recv,
    fan_send,
):
    me = lax.axis_index("seq")
    mine = lax.axis_index("grp")
    pieces = leaving.shape[0]
    own_pieces = prefix_ref.shape[0]
    shares = pieces // own_pieces
    group_pieces = pieces // cb_ref.shape[0]
    spans = cb_ref.shape[1]
    section = x_ref.shape[0]
    last = count - 1
    is_last = me == last
    is_root = me // shares == mine

    barrier = pltpu.get_barrier_semaphore()

    def greet(where):
        pl.semaphore_signal(barrier, inc=1, device_id=where, device_id_type=MESH)

    @pl.when(me > 0)
    def _():
        greet((me - 1, mine))

    @pl.when(me < last)
    def _():
        greet((me + 1, mine))

    for other in range(1, groups):
        greet((me, lax.rem(mine + other, groups)))

    @pl.when(jnp.logical_and(is_root, me < last))
    def _():
        greet((last, mine))

    for share in range(shares):
        owner = mine * shares + share

        @pl.when(jnp.logical_and(is_last, owner != last))
        def _():
            greet((owner, mine))

    expected = (
        (me > 0).astype(jnp.int32)
        + (me < last).astype(jnp.int32)
        + (groups - 1)
        + jnp.logical_and(is_root, me < last).astype(jnp.int32)
    )
    for share in range(shares):
        expected = expected + jnp.logical_and(is_last, mine * shares + share != last).astype(
            jnp.int32
        )
    pl.semaphore_wait(barrier, expected)

    def pass_on(piece, target):
        rows = pl.ds(piece, 1)
        return pltpu.make_async_remote_copy(
            src_ref=leaving.at[rows],
            dst_ref=incoming_ref.at[rows],
            send_sem=send_sem.at[piece],
            recv_sem=recv_sem.at[piece],
            device_id=(target, mine),
            device_id_type=MESH,
        )

    def final_copy(piece, own_piece, owner):
        return pltpu.make_async_remote_copy(
            src_ref=leaving.at[pl.ds(piece, 1)],
            dst_ref=prefix_ref.at[pl.ds(own_piece, 1)],
            send_sem=final_send.at[piece],
            recv_sem=prefix_recv.at[own_piece],
            device_id=(owner, mine),
            device_id_type=MESH,
        )

    def fan_copy(own_piece, other):
        rows = pl.ds(own_piece, 1)
        return pltpu.make_async_remote_copy(
            src_ref=prefix_ref.at[rows],
            dst_ref=prefix_ref.at[rows],
            send_sem=fan_send.at[other - 1, own_piece],
            recv_sem=prefix_recv.at[own_piece],
            device_id=(me, lax.rem(mine + other, groups)),
            device_id_type=MESH,
        )

    left_half = lax.broadcasted_iota(jnp.int32, (SPAN, PAIR), 1) < HDIM
    causal = lax.broadcasted_iota(jnp.int32, (SPAN, SPAN), 0) >= lax.broadcasted_iota(
        jnp.int32, (SPAN, SPAN), 1
    )

    def one_piece(piece, carry):
        group = piece // group_pieces
        columns = pl.ds(pl.multiple_of(piece * PAIR, PAIR), PAIR)
        padded[0:8] = lead_ref[:, columns]
        padded[8 : 8 + section] = x_ref[:, columns].astype(jnp.float32)
        taps = taps_ref[:, columns]
        row_data = rows_ref[piece]
        column_data = row_data.T
        lane_data = lanes_ref[piece]
        gain = lane_data[0:1]
        factor = lane_data[1:2]
        convolved = []
        scaled = []
        growth = []
        updates = []
        for span in range(spans):
            first = span * SPAN
            total = jnp.zeros((SPAN, PAIR), jnp.float32)
            for position in range(TAPS):
                start = 8 - (TAPS - 1) + first + position
                total = total + taps[position : position + 1] * padded[start : start + SPAN]
            value = total / (1.0 + jnp.exp(-total))
            cols = column_data[first : first + SPAN]
            level = jnp.where(left_half, cols[:, 0:1], cols[:, 1:2])
            step = jnp.where(left_half, cols[:, 2:3], cols[:, 3:4])
            closing = lane_data[2 + span : 3 + span]
            inputs = value * step
            convolved.append(value)
            scaled.append(inputs)
            growth.append(jnp.exp(level))
            updates.append(
                dot_split(
                    bt_hi_ref[group, :, first : first + SPAN],
                    bt_lo_ref[group, :, first : first + SPAN],
                    inputs * jnp.exp(closing - level),
                )
            )
        ending = updates[0]
        for span in range(1, spans):
            ending = jnp.exp(lane_data[2 + span : 3 + span]) * ending + updates[span]

        @pl.when(me == 0)
        def _():
            incoming_ref[piece] = jnp.zeros((STATE, PAIR), jnp.float32)

        @pl.when(me > 0)
        def _():
            pass_on(piece, me).wait_recv()

        state = incoming_ref[piece]
        leaving[piece] = factor * state + ending

        @pl.when(me < last)
        def _():
            pass_on(piece, me + 1).start()

        owner = mine * shares + piece // own_pieces
        own_piece = lax.rem(piece, own_pieces)

        @pl.when(jnp.logical_and(is_last, owner != last))
        def _():
            final_copy(piece, own_piece, owner).start()

        @pl.when(jnp.logical_and(is_last, owner == last))
        def _():
            prefix_ref[own_piece] = leaving[piece]
            for other in range(1, groups):
                fan_copy(own_piece, other).start()

        for span in range(spans):
            first = span * SPAN
            carried = growth[span] * dot_split(
                c_hi_ref[group, first : first + SPAN], c_lo_ref[group, first : first + SPAN], state
            )
            halves = []
            for half in range(2):
                fall = (
                    column_data[first : first + SPAN, half : half + 1]
                    - row_data[half : half + 1, first : first + SPAN]
                )
                weights = jnp.exp(jnp.where(causal, fall, NEG)) * cb_ref[group, span]
                hi, lo = split(weights)
                halves.append(dot_split(hi, lo, scaled[span]))
            inside = jnp.where(left_half, halves[0], halves[1])
            y_ref[first : first + SPAN, columns] = (
                inside + carried + gain * convolved[span]
            ).astype(y_ref.dtype)
            state = jnp.exp(lane_data[2 + span : 3 + span]) * state + updates[span]
        return carry

    lax.fori_loop(0, pieces, one_piece, 0)

    def one_arrival(own_piece, carry):
        @pl.when(jnp.logical_not(jnp.logical_and(is_root, is_last)))
        def _():
            final_copy(own_piece, own_piece, me).wait_recv()

        @pl.when(jnp.logical_and(is_root, me < last))
        def _():
            for other in range(1, groups):
                fan_copy(own_piece, other).start()

        return carry

    lax.fori_loop(0, own_pieces, one_arrival, 0)

    def drain(piece, carry):
        owner = mine * shares + piece // own_pieces

        @pl.when(me < last)
        def _():
            pass_on(piece, me).wait_send()

        @pl.when(jnp.logical_and(is_last, owner != last))
        def _():
            final_copy(piece, lax.rem(piece, own_pieces), owner).wait_send()

        return carry

    lax.fori_loop(0, pieces, drain, 0)

    @pl.when(is_root)
    def _():
        def drain_fan(own_piece, carry):
            for other in range(1, groups):
                fan_copy(own_piece, other).wait_send()
            return carry

        lax.fori_loop(0, own_pieces, drain_fan, 0)


def relay_states(operands, own_pieces, count, groups):
    section, width = operands[0].shape
    pieces = width // PAIR
    vmem = pl.BlockSpec(memory_space=pltpu.VMEM)
    return pl.pallas_call(
        functools.partial(relay_kernel, count, groups),
        out_shape=(
            jax.ShapeDtypeStruct((section, width), jnp.bfloat16),
            jax.ShapeDtypeStruct((own_pieces, STATE, PAIR), jnp.float32),
        ),
        in_specs=[vmem] * len(operands),
        out_specs=(vmem, vmem),
        scratch_shapes=[
            pltpu.VMEM((pieces, STATE, PAIR), jnp.float32),
            pltpu.VMEM((pieces, STATE, PAIR), jnp.float32),
            pltpu.VMEM((section + 8, PAIR), jnp.float32),
            pltpu.SemaphoreType.DMA((pieces,)),
            pltpu.SemaphoreType.DMA((pieces,)),
            pltpu.SemaphoreType.DMA((pieces,)),
            pltpu.SemaphoreType.DMA((own_pieces,)),
            pltpu.SemaphoreType.DMA((groups - 1, own_pieces)),
        ],
        compiler_params=pltpu.CompilerParams(
            collective_id=0, has_side_effects=True, vmem_limit_bytes=48 * 1024 * 1024
        ),
    )(*operands)


def on_device(
    pre_x,
    pre_b,
    pre_c,
    pre_dt,
    decay_rate,
    skip_gain,
    conv_taps,
    dec_x,
    dec_b,
    dec_c,
    dec_dt,
    dec_query,
    new_kv,
    cache_kv,
    kv_len,
):
    seq_count = lax.axis_size("seq")
    seq_index = lax.axis_index("seq")
    grp_index = lax.axis_index("grp")
    section = pre_x.shape[0]
    local_heads = pre_x.shape[1] // HDIM
    edge = TAPS - 1
    x_offset = HEADS * HDIM
    c_offset = HEADS * HDIM + GROUPS * STATE
    head_begin = grp_index * local_heads
    group_begin, group_count, heads_each = group_layout(head_begin, local_heads)
    last_x = pre_x[section - edge :].astype(jnp.float32)
    full_b = pre_b.astype(jnp.float32)
    full_c = pre_c.astype(jnp.float32)
    own_b = lax.dynamic_slice_in_dim(full_b, group_begin * STATE, group_count * STATE, 1)
    own_c = lax.dynamic_slice_in_dim(full_c, group_begin * STATE, group_count * STATE, 1)
    edge_rows = jnp.concatenate(
        [last_x, own_b[section - edge :], own_c[section - edge :]], axis=1
    )
    edge_rows = passed_along(edge_rows, "seq", 1)
    split_b = local_heads * HDIM
    split_c = split_b + group_count * STATE
    leading = (edge_rows[:, :split_b], edge_rows[:, split_b:split_c], edge_rows[:, split_c:])
    is_end = seq_index == seq_count - 1
    shown_x = jnp.where(is_end, last_x, 0.0)
    shown_bc = jnp.where(
        jnp.logical_and(is_end, grp_index == 0),
        jnp.concatenate([full_b[section - edge :], full_c[section - edge :]], axis=1),
        0.0,
    )
    tails = jnp.concatenate([jnp.zeros((edge, x_offset), jnp.float32), shown_bc], axis=1)
    tails = lax.dynamic_update_slice_in_dim(tails, shown_x, head_begin * HDIM, 1)
    tails = lax.psum(tails, ("seq", "grp"))
    kernel_x = lax.dynamic_slice_in_dim(conv_taps, head_begin * HDIM, local_heads * HDIM, 1)
    kernel_b = lax.dynamic_slice_in_dim(
        conv_taps, x_offset + group_begin * STATE, group_count * STATE, 1
    )
    kernel_c = lax.dynamic_slice_in_dim(
        conv_taps, c_offset + group_begin * STATE, group_count * STATE, 1
    )
    conv_b = causal_conv(leading[1], own_b, kernel_b)
    conv_c = causal_conv(leading[2], own_c, kernel_c)
    rates = lax.dynamic_slice_in_dim(decay_rate, head_begin, local_heads, 0)
    gains = lax.dynamic_slice_in_dim(skip_gain, head_begin, local_heads, 0)
    spans = section // SPAN
    pieces = local_heads // 2
    log_decay = (-pre_dt * rates[:, None]).reshape(local_heads, spans, SPAN)
    levels = jnp.cumsum(log_decay, axis=2)
    closings = levels[:, :, -1]
    row_data = jnp.concatenate(
        [
            levels.reshape(pieces, 2, section),
            pre_dt.reshape(pieces, 2, section),
            jnp.zeros((pieces, 4, section), jnp.float32),
        ],
        axis=1,
    )
    lane_data = jnp.concatenate(
        [gains[:, None], jnp.exp(jnp.sum(closings, axis=1))[:, None], closings], axis=1
    )
    lane_data = jnp.repeat(
        lane_data.reshape(pieces, 2, spans + 2).transpose(0, 2, 1), HDIM, axis=2
    )
    lane_data = jnp.pad(lane_data, ((0, 0), (0, 6 - spans), (0, 0)))
    entries = conv_b.reshape(section, group_count, STATE).transpose(1, 2, 0)
    readout = conv_c.reshape(section, group_count, STATE).transpose(1, 0, 2)
    crossing = jnp.einsum(
        "gitn,gnis->gits",
        readout.reshape(group_count, spans, SPAN, STATE),
        entries.reshape(group_count, STATE, spans, SPAN),
        precision=HIGH,
    )
    state_heads = HEADS // seq_count
    own_pieces = state_heads // 2
    pre_y, prefix_pairs = relay_states(
        (
            pre_x,
            jnp.pad(leading[0], ((8 - edge, 0), (0, 0))),
            jnp.pad(kernel_x, ((0, 8 - TAPS), (0, 0))),
            row_data,
            lane_data,
            *split_outside(entries),
            *split_outside(readout),
            crossing,
        ),
        own_pieces,
        seq_count,
        lax.axis_size("grp"),
    )
    prefix_tail = lax.dynamic_slice_in_dim(
        tails, seq_index * state_heads * HDIM, state_heads * HDIM, 1
    )
    tail_b = tails[:, x_offset:c_offset]
    tail_c = tails[:, c_offset:]
    rows_here = dec_x.shape[1]
    dec_begin = seq_index * state_heads
    dgroup_begin, dgroup_count, dheads_each = group_layout(dec_begin, state_heads)
    kernel_dx = lax.dynamic_slice_in_dim(conv_taps, dec_begin * HDIM, state_heads * HDIM, 1)
    kernel_db = lax.dynamic_slice_in_dim(
        conv_taps, x_offset + dgroup_begin * STATE, dgroup_count * STATE, 1
    )
    kernel_dc = lax.dynamic_slice_in_dim(
        conv_taps, c_offset + dgroup_begin * STATE, dgroup_count * STATE, 1
    )
    step_x = decode_conv(prefix_tail, dec_x.astype(jnp.float32), kernel_dx)
    step_b = decode_conv(
        lax.dynamic_slice_in_dim(tail_b, dgroup_begin * STATE, dgroup_count * STATE, 1),
        lax.dynamic_slice_in_dim(dec_b, dgroup_begin * STATE, dgroup_count * STATE, 2).astype(
            jnp.float32
        ),
        kernel_db,
    )
    step_c = decode_conv(
        lax.dynamic_slice_in_dim(tail_c, dgroup_begin * STATE, dgroup_count * STATE, 1),
        lax.dynamic_slice_in_dim(dec_c, dgroup_begin * STATE, dgroup_count * STATE, 2).astype(
            jnp.float32
        ),
        kernel_dc,
    )
    heads_x = step_x.reshape(STEPS, rows_here, state_heads, HDIM)
    heads_b = jnp.repeat(step_b.reshape(STEPS, rows_here, dgroup_count, STATE), dheads_each, axis=2)
    heads_c = jnp.repeat(step_c.reshape(STEPS, rows_here, dgroup_count, STATE), dheads_each, axis=2)
    dec_rates = lax.dynamic_slice_in_dim(decay_rate, dec_begin, state_heads, 0)
    dec_gains = lax.dynamic_slice_in_dim(skip_gain, dec_begin, state_heads, 0)
    from_prefix = jnp.einsum(
        "jrgn,gqnl->jrgql",
        step_c.reshape(STEPS, rows_here, dgroup_count, STATE),
        prefix_pairs.reshape(dgroup_count, own_pieces // dgroup_count, STATE, PAIR),
        precision=HIGH,
    ).reshape(STEPS, rows_here, state_heads, HDIM)
    mamba_out = decode_mamba(from_prefix, heads_x, heads_b, heads_c, dec_dt, dec_rates, dec_gains)
    dec_y = mamba_out.reshape(STEPS, rows_here, state_heads * HDIM).astype(jnp.bfloat16)
    group_size = QHEADS // KVHEADS
    score_scale = ADIM ** (-0.5)
    positions = cache_kv.shape[2]
    queries = dec_query.reshape(STEPS, rows_here, KVHEADS, group_size, ADIM)
    key_rows = cache_kv[0].reshape(rows_here, positions, KVHEADS, ADIM)
    value_rows = cache_kv[1].reshape(rows_here, positions, KVHEADS, ADIM).astype(jnp.float32)
    scores = (
        jnp.einsum("jrkgd,rckd->jrkgc", queries, key_rows, preferred_element_type=jnp.float32)
        * score_scale
    )
    places = seq_index * positions + jnp.arange(positions)
    usable = (places[None, :] < kv_len[:, None])[None, :, None, None, :]
    scores = jnp.where(usable, scores, NEG)
    peak_local = jnp.max(scores, axis=-1)
    weights = jnp.where(usable, jnp.exp(scores - peak_local[..., None]), 0.0)
    mass_local = jnp.sum(weights, axis=-1)
    summed_local = jnp.einsum("jrkgc,rckd->jrkgd", weights, value_rows, precision=HIGH)
    peak_local = peak_local.reshape(STEPS, rows_here, QHEADS)
    mass_local = mass_local.reshape(STEPS, rows_here, QHEADS)
    summed_local = summed_local.reshape(STEPS, rows_here, QHEADS, ADIM)
    own_heads = QHEADS // seq_count
    head_start = seq_index * own_heads
    pieces = (
        lax.all_to_all(peak_local[None], "seq", split_axis=3, concat_axis=0, tiled=True),
        lax.all_to_all(mass_local[None], "seq", split_axis=3, concat_axis=0, tiled=True),
        lax.all_to_all(summed_local[None], "seq", split_axis=3, concat_axis=0, tiled=True),
    )
    peak_cache = jnp.max(pieces[0], axis=0)
    rescale = jnp.exp(pieces[0] - peak_cache[None])
    mass_cache = jnp.sum(pieces[1] * rescale, axis=0)
    summed_cache = jnp.sum(pieces[2] * rescale[..., None], axis=0)
    new_keys = new_kv[0].reshape(STEPS, rows_here, KVHEADS, ADIM)
    new_values = new_kv[1].reshape(STEPS, rows_here, KVHEADS, ADIM).astype(jnp.float32)
    new_scores = (
        jnp.einsum("jrkgd,irkd->jrkgi", queries, new_keys, preferred_element_type=jnp.float32)
        * score_scale
    )
    allowed = (jnp.arange(STEPS)[None, :] <= jnp.arange(STEPS)[:, None])[:, None, None, None, :]
    new_scores = jnp.where(allowed, new_scores, NEG)
    new_scores = lax.dynamic_slice_in_dim(
        new_scores.reshape(STEPS, rows_here, QHEADS, STEPS), head_start, own_heads, 2
    )
    allowed_heads = (jnp.arange(STEPS)[None, :] <= jnp.arange(STEPS)[:, None])[:, None, None, :]
    head_kv = (head_start + jnp.arange(own_heads)) // group_size
    pick = (head_kv[:, None] == jnp.arange(KVHEADS)[None, :]).astype(jnp.float32)
    own_values = jnp.einsum("hk,irkd->irhd", pick, new_values, precision=HIGH)
    peak_total = jnp.maximum(peak_cache, jnp.max(new_scores, axis=-1))
    cache_scale = jnp.exp(peak_cache - peak_total)
    new_weights = jnp.where(allowed_heads, jnp.exp(new_scores - peak_total[..., None]), 0.0)
    mass_total = mass_cache * cache_scale + jnp.sum(new_weights, axis=-1)
    summed_total = summed_cache * cache_scale[..., None] + jnp.einsum(
        "jrhi,irhd->jrhd", new_weights, own_values, precision=HIGH
    )
    attn_out = (
        (summed_total / mass_total[..., None])
        .reshape(STEPS, rows_here, own_heads * ADIM)
        .astype(jnp.bfloat16)
    )
    return (pre_y, dec_y, attn_out)


def solution(mesh):
    in_specs = (
        P("seq", "grp"),
        P("seq", None),
        P("seq", None),
        P("grp", "seq"),
        P(),
        P(),
        P(),
        P(None, "grp", "seq"),
        P(None, "grp", None),
        P(None, "grp", None),
        P(None, "grp", "seq"),
        P(None, "grp", None),
        P(None, None, "grp", None),
        P(None, "grp", "seq", None),
        P("grp"),
    )
    out_specs = (P("seq", "grp"), P(None, "grp", "seq"), P(None, "grp", "seq"))
    return jax.shard_map(
        on_device, mesh=mesh, in_specs=in_specs, out_specs=out_specs, check_vma=False
    )
```

```python
import functools

import jax
import jax.numpy as jnp
from jax import lax
from jax.experimental import pallas as pl
from jax.experimental.pallas import tpu as pltpu
from jax.sharding import PartitionSpec as P

HEADS = 256
HDIM = 64
STATE = 256
GROUPS = 8
TAPS = 4
QHEADS = 64
KVHEADS = 8
ADIM = 128
SPAN = 256
STEPS = 2


HIGH = lax.Precision.HIGH
MESH = pl.DeviceIdType.MESH
NEG = -1e30
PAIR = 2 * HDIM


def passed_along(value, axis, steps):
    count = lax.axis_size(axis)
    first, last = (max(0, -steps), min(count, count - steps))
    return lax.ppermute(value, axis, [(source, source + steps) for source in range(first, last)])


def causal_conv(leading, source, kernel):
    row_total = source.shape[0]
    padded = jnp.concatenate([leading, source], axis=0)
    accumulated = jnp.zeros_like(source)
    for position in range(TAPS):
        accumulated = accumulated + kernel[position] * padded[position : position + row_total]
    return jax.nn.silu(accumulated)


def decode_conv(leading, fresh, kernel):
    results = []
    for current in range(fresh.shape[0]):
        accumulated = jnp.zeros(fresh.shape[1:], jnp.float32)
        for position in range(TAPS):
            place = current + position
            if place < TAPS - 1:
                term = leading[place][None, :]
            else:
                term = fresh[place - (TAPS - 1)]
            accumulated = accumulated + kernel[position] * term
        results.append(jax.nn.silu(accumulated))
    return jnp.stack(results)


def decode_mamba(from_prefix, heads_x, heads_b, heads_c, step_dt, rates, gains):
    decays = jnp.exp(-step_dt * rates)
    results = []
    for current in range(heads_x.shape[0]):
        factor = jnp.ones(decays.shape[1:], jnp.float32)
        accumulated = gains[None, :, None] * heads_x[current]
        for earlier in range(current, -1, -1):
            intersection = jnp.sum(heads_c[current] * heads_b[earlier], axis=-1)
            accumulated = (
                accumulated
                + (factor * step_dt[earlier] * intersection)[..., None] * heads_x[earlier]
            )
            factor = factor * decays[earlier]
        accumulated = accumulated + factor[..., None] * from_prefix[current]
        results.append(accumulated)
    return jnp.stack(results)


def group_layout(head_begin, head_count):
    per_group = HEADS // GROUPS
    group_count = max(1, head_count // per_group)
    return (head_begin // per_group, group_count, head_count // group_count)


def split(value):
    hi = value.astype(jnp.bfloat16)
    return hi, (value - hi.astype(jnp.float32)).astype(jnp.bfloat16)


def split_outside(value):
    hi = lax.reduce_precision(value, 8, 7)
    return hi.astype(jnp.bfloat16), (value - hi).astype(jnp.bfloat16)


def dot_split(hi, lo, right):
    right_hi, right_lo = split(right)
    width = right.shape[1]
    both = jnp.dot(
        hi,
        jnp.concatenate([right_hi, right_lo], axis=1),
        preferred_element_type=jnp.float32,
    )
    small = jnp.dot(lo, right_hi, preferred_element_type=jnp.float32)
    return both[:, :width] + (both[:, width:] + small)


def relay_kernel(
    count,
    groups,
    x_ref,
    lead_ref,
    taps_ref,
    rows_ref,
    lanes_ref,
    bt_hi_ref,
    bt_lo_ref,
    c_hi_ref,
    c_lo_ref,
    cb_ref,
    y_ref,
    prefix_ref,
    incoming_ref,
    leaving,
    padded,
    send_sem,
    recv_sem,
    final_send,
    prefix_recv,
    fan_send,
):
    me = lax.axis_index("seq")
    mine = lax.axis_index("grp")
    pieces = leaving.shape[0]
    own_pieces = prefix_ref.shape[0]
    shares = pieces // own_pieces
    group_pieces = pieces // cb_ref.shape[0]
    spans = cb_ref.shape[1]
    section = x_ref.shape[0]
    last = count - 1
    is_last = me == last
    is_root = me // shares == mine
    hands_on = lax.rem(me // shares, 2) == lax.rem(mine, 2)
    sibling = mine + 1 - 2 * lax.rem(mine, 2)

    barrier = pltpu.get_barrier_semaphore()

    def greet(where):
        pl.semaphore_signal(barrier, inc=1, device_id=where, device_id_type=MESH)

    @pl.when(me > 0)
    def _():
        greet((me - 1, mine))

    @pl.when(me < last)
    def _():
        greet((me + 1, mine))

    for other in range(1, groups):
        greet((me, lax.rem(mine + other, groups)))

    @pl.when(jnp.logical_and(is_root, me < last))
    def _():
        greet((last, mine))

    for share in range(shares):
        owner = mine * shares + share

        @pl.when(jnp.logical_and(is_last, owner != last))
        def _():
            greet((owner, mine))

    expected = (
        (me > 0).astype(jnp.int32)
        + (me < last).astype(jnp.int32)
        + (groups - 1)
        + jnp.logical_and(is_root, me < last).astype(jnp.int32)
    )
    for share in range(shares):
        expected = expected + jnp.logical_and(is_last, mine * shares + share != last).astype(
            jnp.int32
        )
    pl.semaphore_wait(barrier, expected)

    def pass_on(piece, target):
        rows = pl.ds(piece, 1)
        return pltpu.make_async_remote_copy(
            src_ref=leaving.at[rows],
            dst_ref=incoming_ref.at[rows],
            send_sem=send_sem.at[piece],
            recv_sem=recv_sem.at[piece],
            device_id=(target, mine),
            device_id_type=MESH,
        )

    def final_copy(piece, own_piece, owner):
        return pltpu.make_async_remote_copy(
            src_ref=leaving.at[pl.ds(piece, 1)],
            dst_ref=prefix_ref.at[pl.ds(own_piece, 1)],
            send_sem=final_send.at[piece],
            recv_sem=prefix_recv.at[own_piece],
            device_id=(owner, mine),
            device_id_type=MESH,
        )

    def fan_copy(own_piece, other):
        rows = pl.ds(own_piece, 1)
        return pltpu.make_async_remote_copy(
            src_ref=prefix_ref.at[rows],
            dst_ref=prefix_ref.at[rows],
            send_sem=fan_send.at[other - 1, own_piece],
            recv_sem=prefix_recv.at[own_piece],
            device_id=(me, lax.rem(mine + other, groups)),
            device_id_type=MESH,
        )

    def sibling_copy(own_piece):
        rows = pl.ds(own_piece, 1)
        return pltpu.make_async_remote_copy(
            src_ref=prefix_ref.at[rows],
            dst_ref=prefix_ref.at[rows],
            send_sem=fan_send.at[0, own_piece],
            recv_sem=prefix_recv.at[own_piece],
            device_id=(me, sibling),
            device_id_type=MESH,
        )

    left_half = lax.broadcasted_iota(jnp.int32, (SPAN, PAIR), 1) < HDIM
    causal = lax.broadcasted_iota(jnp.int32, (SPAN, SPAN), 0) >= lax.broadcasted_iota(
        jnp.int32, (SPAN, SPAN), 1
    )

    def one_piece(piece, carry):
        group = piece // group_pieces
        columns = pl.ds(pl.multiple_of(piece * PAIR, PAIR), PAIR)
        padded[0:8] = lead_ref[:, columns]
        padded[8 : 8 + section] = x_ref[:, columns].astype(jnp.float32)
        taps = taps_ref[:, columns]
        row_data = rows_ref[piece]
        column_data = row_data.T
        lane_data = lanes_ref[piece]
        gain = lane_data[0:1]
        factor = lane_data[1:2]
        convolved = []
        scaled = []
        growth = []
        updates = []
        for span in range(spans):
            first = span * SPAN
            total = jnp.zeros((SPAN, PAIR), jnp.float32)
            for position in range(TAPS):
                start = 8 - (TAPS - 1) + first + position
                total = total + taps[position : position + 1] * padded[start : start + SPAN]
            value = total / (1.0 + jnp.exp(-total))
            cols = column_data[first : first + SPAN]
            level = jnp.where(left_half, cols[:, 0:1], cols[:, 1:2])
            step = jnp.where(left_half, cols[:, 2:3], cols[:, 3:4])
            closing = lane_data[2 + span : 3 + span]
            inputs = value * step
            convolved.append(value)
            scaled.append(inputs)
            growth.append(jnp.exp(level))
            updates.append(
                dot_split(
                    bt_hi_ref[group, :, first : first + SPAN],
                    bt_lo_ref[group, :, first : first + SPAN],
                    inputs * jnp.exp(closing - level),
                )
            )
        ending = updates[0]
        for span in range(1, spans):
            ending = jnp.exp(lane_data[2 + span : 3 + span]) * ending + updates[span]

        @pl.when(me == 0)
        def _():
            incoming_ref[piece] = jnp.zeros((STATE, PAIR), jnp.float32)

        @pl.when(me > 0)
        def _():
            pass_on(piece, me).wait_recv()

        state = incoming_ref[piece]
        leaving[piece] = factor * state + ending

        @pl.when(me < last)
        def _():
            pass_on(piece, me + 1).start()

        owner = mine * shares + piece // own_pieces
        own_piece = lax.rem(piece, own_pieces)

        @pl.when(jnp.logical_and(is_last, owner != last))
        def _():
            final_copy(piece, own_piece, owner).start()

        @pl.when(jnp.logical_and(is_last, owner == last))
        def _():
            prefix_ref[own_piece] = leaving[piece]
            for other in range(2, groups, 2):
                fan_copy(own_piece, other).start()
            sibling_copy(own_piece).start()

        for span in range(spans):
            first = span * SPAN
            carried = growth[span] * dot_split(
                c_hi_ref[group, first : first + SPAN], c_lo_ref[group, first : first + SPAN], state
            )
            halves = []
            for half in range(2):
                fall = (
                    column_data[first : first + SPAN, half : half + 1]
                    - row_data[half : half + 1, first : first + SPAN]
                )
                weights = jnp.exp(jnp.where(causal, fall, NEG)) * cb_ref[group, span]
                hi, lo = split(weights)
                halves.append(dot_split(hi, lo, scaled[span]))
            inside = jnp.where(left_half, halves[0], halves[1])
            y_ref[first : first + SPAN, columns] = (
                inside + carried + gain * convolved[span]
            ).astype(y_ref.dtype)
            state = jnp.exp(lane_data[2 + span : 3 + span]) * state + updates[span]
        return carry

    lax.fori_loop(0, pieces, one_piece, 0)

    def one_arrival(own_piece, carry):
        @pl.when(jnp.logical_not(jnp.logical_and(is_root, is_last)))
        def _():
            final_copy(own_piece, own_piece, me).wait_recv()

        @pl.when(jnp.logical_and(is_root, me < last))
        def _():
            for other in range(2, groups, 2):
                fan_copy(own_piece, other).start()

        @pl.when(jnp.logical_and(hands_on, jnp.logical_not(jnp.logical_and(is_root, is_last))))
        def _():
            sibling_copy(own_piece).start()

        return carry

    lax.fori_loop(0, own_pieces, one_arrival, 0)

    def drain(piece, carry):
        owner = mine * shares + piece // own_pieces

        @pl.when(me < last)
        def _():
            pass_on(piece, me).wait_send()

        @pl.when(jnp.logical_and(is_last, owner != last))
        def _():
            final_copy(piece, lax.rem(piece, own_pieces), owner).wait_send()

        return carry

    lax.fori_loop(0, pieces, drain, 0)

    @pl.when(is_root)
    def _():
        def drain_fan(own_piece, carry):
            for other in range(2, groups, 2):
                fan_copy(own_piece, other).wait_send()
            return carry

        lax.fori_loop(0, own_pieces, drain_fan, 0)

    @pl.when(hands_on)
    def _():
        def drain_sibling(own_piece, carry):
            sibling_copy(own_piece).wait_send()
            return carry

        lax.fori_loop(0, own_pieces, drain_sibling, 0)


def relay_states(operands, own_pieces, count, groups):
    section, width = operands[0].shape
    pieces = width // PAIR
    vmem = pl.BlockSpec(memory_space=pltpu.VMEM)
    return pl.pallas_call(
        functools.partial(relay_kernel, count, groups),
        out_shape=(
            jax.ShapeDtypeStruct((section, width), jnp.bfloat16),
            jax.ShapeDtypeStruct((own_pieces, STATE, PAIR), jnp.float32),
        ),
        in_specs=[vmem] * len(operands),
        out_specs=(vmem, vmem),
        scratch_shapes=[
            pltpu.VMEM((pieces, STATE, PAIR), jnp.float32),
            pltpu.VMEM((pieces, STATE, PAIR), jnp.float32),
            pltpu.VMEM((section + 8, PAIR), jnp.float32),
            pltpu.SemaphoreType.DMA((pieces,)),
            pltpu.SemaphoreType.DMA((pieces,)),
            pltpu.SemaphoreType.DMA((pieces,)),
            pltpu.SemaphoreType.DMA((own_pieces,)),
            pltpu.SemaphoreType.DMA((groups - 1, own_pieces)),
        ],
        compiler_params=pltpu.CompilerParams(
            collective_id=0, has_side_effects=True, vmem_limit_bytes=48 * 1024 * 1024
        ),
    )(*operands)


def on_device(
    pre_x,
    pre_b,
    pre_c,
    pre_dt,
    decay_rate,
    skip_gain,
    conv_taps,
    dec_x,
    dec_b,
    dec_c,
    dec_dt,
    dec_query,
    new_kv,
    cache_kv,
    kv_len,
):
    seq_count = lax.axis_size("seq")
    seq_index = lax.axis_index("seq")
    grp_index = lax.axis_index("grp")
    section = pre_x.shape[0]
    local_heads = pre_x.shape[1] // HDIM
    edge = TAPS - 1
    x_offset = HEADS * HDIM
    c_offset = HEADS * HDIM + GROUPS * STATE
    head_begin = grp_index * local_heads
    group_begin, group_count, heads_each = group_layout(head_begin, local_heads)
    last_x = pre_x[section - edge :].astype(jnp.float32)
    full_b = pre_b.astype(jnp.float32)
    full_c = pre_c.astype(jnp.float32)
    own_b = lax.dynamic_slice_in_dim(full_b, group_begin * STATE, group_count * STATE, 1)
    own_c = lax.dynamic_slice_in_dim(full_c, group_begin * STATE, group_count * STATE, 1)
    edge_rows = jnp.concatenate(
        [last_x, own_b[section - edge :], own_c[section - edge :]], axis=1
    )
    edge_rows = passed_along(edge_rows, "seq", 1)
    split_b = local_heads * HDIM
    split_c = split_b + group_count * STATE
    leading = (edge_rows[:, :split_b], edge_rows[:, split_b:split_c], edge_rows[:, split_c:])
    is_end = seq_index == seq_count - 1
    shown_x = jnp.where(is_end, last_x, 0.0)
    shown_bc = jnp.where(
        jnp.logical_and(is_end, grp_index == 0),
        jnp.concatenate([full_b[section - edge :], full_c[section - edge :]], axis=1),
        0.0,
    )
    tails = jnp.concatenate([jnp.zeros((edge, x_offset), jnp.float32), shown_bc], axis=1)
    tails = lax.dynamic_update_slice_in_dim(tails, shown_x, head_begin * HDIM, 1)
    tails = lax.psum(tails, ("seq", "grp"))
    kernel_x = lax.dynamic_slice_in_dim(conv_taps, head_begin * HDIM, local_heads * HDIM, 1)
    kernel_b = lax.dynamic_slice_in_dim(
        conv_taps, x_offset + group_begin * STATE, group_count * STATE, 1
    )
    kernel_c = lax.dynamic_slice_in_dim(
        conv_taps, c_offset + group_begin * STATE, group_count * STATE, 1
    )
    conv_b = causal_conv(leading[1], own_b, kernel_b)
    conv_c = causal_conv(leading[2], own_c, kernel_c)
    rates = lax.dynamic_slice_in_dim(decay_rate, head_begin, local_heads, 0)
    gains = lax.dynamic_slice_in_dim(skip_gain, head_begin, local_heads, 0)
    spans = section // SPAN
    pieces = local_heads // 2
    log_decay = (-pre_dt * rates[:, None]).reshape(local_heads, spans, SPAN)
    levels = jnp.cumsum(log_decay, axis=2)
    closings = levels[:, :, -1]
    row_data = jnp.concatenate(
        [
            levels.reshape(pieces, 2, section),
            pre_dt.reshape(pieces, 2, section),
            jnp.zeros((pieces, 4, section), jnp.float32),
        ],
        axis=1,
    )
    lane_data = jnp.concatenate(
        [gains[:, None], jnp.exp(jnp.sum(closings, axis=1))[:, None], closings], axis=1
    )
    lane_data = jnp.repeat(
        lane_data.reshape(pieces, 2, spans + 2).transpose(0, 2, 1), HDIM, axis=2
    )
    lane_data = jnp.pad(lane_data, ((0, 0), (0, 6 - spans), (0, 0)))
    entries = conv_b.reshape(section, group_count, STATE).transpose(1, 2, 0)
    readout = conv_c.reshape(section, group_count, STATE).transpose(1, 0, 2)
    crossing = jnp.einsum(
        "gitn,gnis->gits",
        readout.reshape(group_count, spans, SPAN, STATE),
        entries.reshape(group_count, STATE, spans, SPAN),
        precision=HIGH,
    )
    state_heads = HEADS // seq_count
    own_pieces = state_heads // 2
    pre_y, prefix_pairs = relay_states(
        (
            pre_x,
            jnp.pad(leading[0], ((8 - edge, 0), (0, 0))),
            jnp.pad(kernel_x, ((0, 8 - TAPS), (0, 0))),
            row_data,
            lane_data,
            *split_outside(entries),
            *split_outside(readout),
            crossing,
        ),
        own_pieces,
        seq_count,
        lax.axis_size("grp"),
    )
    prefix_tail = lax.dynamic_slice_in_dim(
        tails, seq_index * state_heads * HDIM, state_heads * HDIM, 1
    )
    tail_b = tails[:, x_offset:c_offset]
    tail_c = tails[:, c_offset:]
    rows_here = dec_x.shape[1]
    dec_begin = seq_index * state_heads
    dgroup_begin, dgroup_count, dheads_each = group_layout(dec_begin, state_heads)
    kernel_dx = lax.dynamic_slice_in_dim(conv_taps, dec_begin * HDIM, state_heads * HDIM, 1)
    kernel_db = lax.dynamic_slice_in_dim(
        conv_taps, x_offset + dgroup_begin * STATE, dgroup_count * STATE, 1
    )
    kernel_dc = lax.dynamic_slice_in_dim(
        conv_taps, c_offset + dgroup_begin * STATE, dgroup_count * STATE, 1
    )
    step_x = decode_conv(prefix_tail, dec_x.astype(jnp.float32), kernel_dx)
    step_b = decode_conv(
        lax.dynamic_slice_in_dim(tail_b, dgroup_begin * STATE, dgroup_count * STATE, 1),
        lax.dynamic_slice_in_dim(dec_b, dgroup_begin * STATE, dgroup_count * STATE, 2).astype(
            jnp.float32
        ),
        kernel_db,
    )
    step_c = decode_conv(
        lax.dynamic_slice_in_dim(tail_c, dgroup_begin * STATE, dgroup_count * STATE, 1),
        lax.dynamic_slice_in_dim(dec_c, dgroup_begin * STATE, dgroup_count * STATE, 2).astype(
            jnp.float32
        ),
        kernel_dc,
    )
    heads_x = step_x.reshape(STEPS, rows_here, state_heads, HDIM)
    heads_b = jnp.repeat(step_b.reshape(STEPS, rows_here, dgroup_count, STATE), dheads_each, axis=2)
    heads_c = jnp.repeat(step_c.reshape(STEPS, rows_here, dgroup_count, STATE), dheads_each, axis=2)
    dec_rates = lax.dynamic_slice_in_dim(decay_rate, dec_begin, state_heads, 0)
    dec_gains = lax.dynamic_slice_in_dim(skip_gain, dec_begin, state_heads, 0)
    from_prefix = jnp.einsum(
        "jrgn,gqnl->jrgql",
        step_c.reshape(STEPS, rows_here, dgroup_count, STATE),
        prefix_pairs.reshape(dgroup_count, own_pieces // dgroup_count, STATE, PAIR),
        precision=HIGH,
    ).reshape(STEPS, rows_here, state_heads, HDIM)
    mamba_out = decode_mamba(from_prefix, heads_x, heads_b, heads_c, dec_dt, dec_rates, dec_gains)
    dec_y = mamba_out.reshape(STEPS, rows_here, state_heads * HDIM).astype(jnp.bfloat16)
    group_size = QHEADS // KVHEADS
    score_scale = ADIM ** (-0.5)
    positions = cache_kv.shape[2]
    queries = dec_query.reshape(STEPS, rows_here, KVHEADS, group_size, ADIM)
    key_rows = cache_kv[0].reshape(rows_here, positions, KVHEADS, ADIM)
    value_rows = cache_kv[1].reshape(rows_here, positions, KVHEADS, ADIM).astype(jnp.float32)
    scores = (
        jnp.einsum("jrkgd,rckd->jrkgc", queries, key_rows, preferred_element_type=jnp.float32)
        * score_scale
    )
    places = seq_index * positions + jnp.arange(positions)
    usable = (places[None, :] < kv_len[:, None])[None, :, None, None, :]
    scores = jnp.where(usable, scores, NEG)
    peak_local = jnp.max(scores, axis=-1)
    weights = jnp.where(usable, jnp.exp(scores - peak_local[..., None]), 0.0)
    mass_local = jnp.sum(weights, axis=-1)
    summed_local = jnp.einsum("jrkgc,rckd->jrkgd", weights, value_rows, precision=HIGH)
    peak_local = peak_local.reshape(STEPS, rows_here, QHEADS)
    mass_local = mass_local.reshape(STEPS, rows_here, QHEADS)
    summed_local = summed_local.reshape(STEPS, rows_here, QHEADS, ADIM)
    own_heads = QHEADS // seq_count
    head_start = seq_index * own_heads
    lane = jnp.arange(ADIM)
    marks = jnp.where(
        lane == 0, peak_local[..., None], jnp.where(lane == 1, mass_local[..., None], 0.0)
    )
    partials = lax.all_to_all(
        jnp.stack([summed_local, marks])[None], "seq", split_axis=4, concat_axis=0, tiled=True
    )
    pieces = (partials[:, 1, ..., 0], partials[:, 1, ..., 1], partials[:, 0])
    peak_cache = jnp.max(pieces[0], axis=0)
    rescale = jnp.exp(pieces[0] - peak_cache[None])
    mass_cache = jnp.sum(pieces[1] * rescale, axis=0)
    summed_cache = jnp.sum(pieces[2] * rescale[..., None], axis=0)
    new_keys = new_kv[0].reshape(STEPS, rows_here, KVHEADS, ADIM)
    new_values = new_kv[1].reshape(STEPS, rows_here, KVHEADS, ADIM).astype(jnp.float32)
    new_scores = (
        jnp.einsum("jrkgd,irkd->jrkgi", queries, new_keys, preferred_element_type=jnp.float32)
        * score_scale
    )
    allowed = (jnp.arange(STEPS)[None, :] <= jnp.arange(STEPS)[:, None])[:, None, None, None, :]
    new_scores = jnp.where(allowed, new_scores, NEG)
    new_scores = lax.dynamic_slice_in_dim(
        new_scores.reshape(STEPS, rows_here, QHEADS, STEPS), head_start, own_heads, 2
    )
    allowed_heads = (jnp.arange(STEPS)[None, :] <= jnp.arange(STEPS)[:, None])[:, None, None, :]
    head_kv = (head_start + jnp.arange(own_heads)) // group_size
    pick = (head_kv[:, None] == jnp.arange(KVHEADS)[None, :]).astype(jnp.float32)
    own_values = jnp.einsum("hk,irkd->irhd", pick, new_values, precision=HIGH)
    peak_total = jnp.maximum(peak_cache, jnp.max(new_scores, axis=-1))
    cache_scale = jnp.exp(peak_cache - peak_total)
    new_weights = jnp.where(allowed_heads, jnp.exp(new_scores - peak_total[..., None]), 0.0)
    mass_total = mass_cache * cache_scale + jnp.sum(new_weights, axis=-1)
    summed_total = summed_cache * cache_scale[..., None] + jnp.einsum(
        "jrhi,irhd->jrhd", new_weights, own_values, precision=HIGH
    )
    attn_out = (
        (summed_total / mass_total[..., None])
        .reshape(STEPS, rows_here, own_heads * ADIM)
        .astype(jnp.bfloat16)
    )
    return (pre_y, dec_y, attn_out)


def solution(mesh):
    in_specs = (
        P("seq", "grp"),
        P("seq", None),
        P("seq", None),
        P("grp", "seq"),
        P(),
        P(),
        P(),
        P(None, "grp", "seq"),
        P(None, "grp", None),
        P(None, "grp", None),
        P(None, "grp", "seq"),
        P(None, "grp", None),
        P(None, None, "grp", None),
        P(None, "grp", "seq", None),
        P("grp"),
    )
    out_specs = (P("seq", "grp"), P(None, "grp", "seq"), P(None, "grp", "seq"))
    return jax.shard_map(
        on_device, mesh=mesh, in_specs=in_specs, out_specs=out_specs, check_vma=False
    )
```
